512 devices in a mesh: dp: 16 (over z, x_hi), tensor: 32 (over x_lo, y, core).
Axes of the slice: x: 4 (x_hi: 2, x_lo: 2; x = x_hi * 2 + x_lo), y: 8, z: 8, core: 2. Of those that a mesh axis runs over, the one named last changes fastest.
Arguments:
- inputs: bfloat16 [4096, 2304], P(('dp', 'tensor')), may hold values from -6 to 6
- hidden_grad: bfloat16 [4096, 18432], P('dp', 'tensor'), may hold values from -6 to 6
- token_key: int32 [4096], P('dp'), may hold values from 0 to 16777215
- feature_key: int32 [18432], P('tensor'), may hold values from 0 to 16777215
- drop_seed: int32 [1], replicated, may hold values from 0 to 16777215
- gate_weight: bfloat16 [2304, 18432], P('dp', 'tensor'), may hold values from -0.125 to 0.125
- up_weight: bfloat16 [2304, 18432], P('dp', 'tensor'), may hold values from -0.125 to 0.125
- gate_first: float32 [2304, 18432], P('dp', 'tensor'), may hold values from -6 to 6
- gate_second: float32 [2304, 18432], P('dp', 'tensor'), may hold values from 1 to 100
- up_first: float32 [2304, 18432], P('dp', 'tensor'), may hold values from -6 to 6
- up_second: float32 [2304, 18432], P('dp', 'tensor'), may hold values from 1 to 100
Outputs:
- input_grad: bfloat16 [4096, 2304], P(('dp', 'tensor'))
- gate_updated: bfloat16 [2304, 18432], P('dp', 'tensor')
- up_updated: bfloat16 [2304, 18432], P('dp', 'tensor')
- gate_first_new: float32 [2304, 18432], P('dp', 'tensor')
- gate_second_new: float32 [2304, 18432], P('dp', 'tensor')
- up_first_new: float32 [2304, 18432], P('dp', 'tensor')
- up_second_new: float32 [2304, 18432], P('dp', 'tensor')
The draws below stay inside these ranges and needn't reach their ends.
All inputs are finite; a program needn't handle non-finite values.
Results may differ from the reference program's by a relative error of at most 0.0049.
Values may be sent and summed in bfloat16 or wider, within the bound.
No kernel may reach another device: no remote copies, remote signals or barrier semaphores. Data moves between devices by JAX's collectives and lax.ppermute only.
A program may use at most 128 MiB of HBM per device.

```python
import math
import jax
import jax.numpy as jnp

D = 2304
FF = 18432
TOKENS = 4096


def set_ends(drawn, own_key, low, top_value):
    longest = drawn.shape.index(max(drawn.shape))
    spots = []
    for shift in (0, 1):
        where = [jax.random.randint(jax.random.fold_in(own_key, axis), (), 0, length) for axis, length in enumerate(drawn.shape)]
        where[longest] = (where[longest] + shift) % drawn.shape[longest]
        spots.append(tuple(where))
    return drawn.at[spots[0]].set(low).at[spots[1]].set(top_value)


def level_of(own_key, shape, split, least, largest):
    level = 1.0
    for position, parts in split:
        steps = jax.random.uniform(jax.random.fold_in(jax.random.fold_in(own_key, 6), position), (parts,), jnp.float32, least / len(split), largest / len(split))
        level = level * jnp.repeat(jnp.exp(steps), shape[position] // parts).reshape((-1,) + (1,) * (len(shape) - 1 - position))
    return level


def gaussian(own_key, shape, scale, reach, split=(), held_as=jnp.bfloat16):
    level = level_of(own_key, shape, split, -0.22, 0.18) if split else 1.0
    drawn = jax.random.normal(own_key, shape, jnp.float32) * scale * level
    return jnp.minimum(jnp.maximum(drawn, -reach), reach).astype(held_as)


def setup_inputs(seed: int = 0) -> dict:
    key_of = jax.random.split(jax.random.key(seed), 12)
    inputs = gaussian(key_of[0], (TOKENS, D), 1.0, 6.0, ((0, 512),))
    hidden_grad = gaussian(key_of[1], (TOKENS, FF), 1.0, 6.0, ((0, 16), (1, 32)))
    token_key = set_ends(jax.random.randint(key_of[2], (TOKENS,), 0, 16777216), jax.random.fold_in(key_of[2], 1), 0, 16777215).astype(jnp.int32)
    feature_key = set_ends(jax.random.randint(key_of[3], (FF,), 0, 16777216), jax.random.fold_in(key_of[3], 1), 0, 16777215).astype(jnp.int32)
    drop_seed = jax.random.randint(key_of[4], (1,), 0, 16777216).astype(jnp.int32)
    gate_weight = gaussian(key_of[5], (D, FF), D ** -0.5, 0.125, ((0, 16), (1, 32)))
    up_weight = gaussian(key_of[6], (D, FF), D ** -0.5, 0.125, ((0, 16), (1, 32)))
    gate_first = gaussian(key_of[7], (D, FF), 1.0, 6.0, ((0, 16), (1, 32)), jnp.float32)
    gate_second = jnp.clip(jnp.exp(math.log(100.0) - 4.6051702 * jax.random.uniform(key_of[8], (D, FF), jnp.float32) ** level_of(key_of[8], (D, FF), ((0, 16), (1, 32)), -0.2, 0.2)), 1.0, 100.0)
    up_first = gaussian(key_of[9], (D, FF), 1.0, 6.0, ((0, 16), (1, 32)), jnp.float32)
    up_second = jnp.clip(jnp.exp(math.log(100.0) - 4.6051702 * jax.random.uniform(key_of[10], (D, FF), jnp.float32) ** level_of(key_of[10], (D, FF), ((0, 16), (1, 32)), -0.2, 0.2)), 1.0, 100.0)
    return dict(inputs=inputs, hidden_grad=hidden_grad, token_key=token_key, feature_key=feature_key, drop_seed=drop_seed, gate_weight=gate_weight, up_weight=up_weight, gate_first=gate_first, gate_second=gate_second, up_first=up_first, up_second=up_second)


drop_level = 6554
keep_scale = 65536.0 / (65536.0 - 6554.0)
gelu_coeff = math.sqrt(2.0 / math.pi)
first_fix = 1.0 - 0.9 ** 10
second_fix = 1.0 - 0.95 ** 10

def keep_factor(token_key, feature_key, drop_seed):
    mixed = token_key[:, None] * -1640531535 + feature_key[None, :] * -1028477379 + drop_seed[0] * 668265263
    mixed = mixed ^ mixed >> 15 & 131071
    mixed = mixed * -2048144789
    mixed = mixed ^ mixed >> 13 & 524287
    mixed = mixed * -1028477387
    mixed = mixed ^ mixed >> 16 & 65535
    level = mixed & 65535
    return jnp.where(level >= drop_level, jnp.float32(keep_scale), jnp.float32(0.0)).astype(jnp.float32)

def adamw(weight, first, second, grad):
    first_new = 0.9 * first + 0.1 * grad
    second_new = 0.95 * second + 0.05 * grad * grad
    wide = weight.astype(jnp.float32)
    step = first_new / first_fix / (jnp.sqrt(second_new / second_fix) + 1e-08) + 0.1 * wide
    return ((wide - 0.01 * step).astype(jnp.bfloat16), first_new, second_new)

def reference(inputs, hidden_grad, token_key, feature_key, drop_seed, gate_weight, up_weight, gate_first, gate_second, up_first, up_second):
    gate = jnp.dot(inputs, gate_weight, preferred_element_type=jnp.float32)
    up = jnp.dot(inputs, up_weight, preferred_element_type=jnp.float32)
    keep = keep_factor(token_key, feature_key, drop_seed)
    tanh_part = jnp.tanh(gelu_coeff * (gate + 0.044715 * gate * gate * gate))
    act = 0.5 * gate * (1.0 + tanh_part)
    slope = 0.5 * (1.0 + tanh_part) + 0.5 * gate * (1.0 - tanh_part * tanh_part) * gelu_coeff * (1.0 + 3.0 * 0.044715 * gate * gate)
    dropped = hidden_grad.astype(jnp.float32) * keep
    dgate = (dropped * up * slope).astype(jnp.bfloat16)
    dup = (dropped * act).astype(jnp.bfloat16)
    input_grad = (jnp.dot(dgate, gate_weight.T, preferred_element_type=jnp.float32) + jnp.dot(dup, up_weight.T, preferred_element_type=jnp.float32)).astype(jnp.bfloat16)
    grad_gate = jnp.dot(inputs.T, dgate, preferred_element_type=jnp.float32)
    grad_up = jnp.dot(inputs.T, dup, preferred_element_type=jnp.float32)
    gate_updated, gate_first_new, gate_second_new = adamw(gate_weight, gate_first, gate_second, grad_gate)
    up_updated, up_first_new, up_second_new = adamw(up_weight, up_first, up_second, grad_up)
    return (input_grad, gate_updated, up_updated, gate_first_new, gate_second_new, up_first_new, up_second_new)
```

```python
import math

import jax
import jax.numpy as jnp
from jax import lax
from jax.sharding import Mesh
from jax.sharding import PartitionSpec as P

drop_level = 6554
keep_scale = 65536.0 / (65536.0 - 6554.0)
gelu_coeff = math.sqrt(2.0 / math.pi)
first_fix = 1.0 - 0.9**10
second_fix = 1.0 - 0.95**10
bf16 = jnp.bfloat16
f32 = jnp.float32

plane = ("xh", "xl", "y")


def keep_mask(token_key, feature_key, drop_seed):
    mixed = (
        token_key[:, None] * -1640531535
        + feature_key[None, :] * -1028477379
        + drop_seed[0] * 668265263
    )
    mixed = mixed ^ mixed >> 15 & 131071
    mixed = mixed * -2048144789
    mixed = mixed ^ mixed >> 13 & 524287
    mixed = mixed * -1028477387
    mixed = mixed ^ mixed >> 16 & 65535
    level = mixed & 65535
    return level >= drop_level


def adamw(weight, first, second, grad):
    first_new = 0.9 * first + 0.1 * grad
    second_new = 0.95 * second + 0.05 * grad * grad
    wide = weight.astype(f32)
    step = first_new / first_fix / (jnp.sqrt(second_new / second_fix) + 1e-08) + 0.1 * wide
    return ((wide - 0.01 * step).astype(bf16), first_new, second_new)


def swap(x, axis):
    return lax.ppermute(x, axis, [(0, 1), (1, 0)])


def pick(index, first, second):
    return jnp.where(index == 0, first, second), jnp.where(index == 0, second, first)


def ring_sum(terms, axis):
    count = terms.shape[0]
    place = lax.axis_index(axis)
    right = [(i, (i + 1) % count) for i in range(count)]
    left = [(i, (i - 1) % count) for i in range(count)]

    def term(step):
        return lax.dynamic_index_in_dim(terms, lax.rem(place + step + count, count), 0, False)

    ahead, behind = count // 2, count - 1 - count // 2
    rightward, leftward = term(ahead), term(-behind) if behind else 0.0
    for step in range(ahead - 1, -1, -1):
        rightward = lax.ppermute(rightward.astype(bf16), axis, right).astype(f32)
        if step:
            rightward = rightward + term(step)
        if step <= behind - 1:
            leftward = lax.ppermute(leftward.astype(bf16), axis, left).astype(f32)
            if step:
                leftward = leftward + term(-step)
    return rightward + leftward + term(0)


def on_device(
    inputs,
    hidden_grad,
    token_key,
    feature_key,
    drop_seed,
    gate_weight,
    up_weight,
    gate_first,
    gate_second,
    up_first,
    up_second,
):
    xh = lax.axis_index("xh")
    core = lax.axis_index("core")
    own_rows, own_units = gate_weight.shape
    half = own_units // 2
    model = inputs.shape[1]
    own_inputs = inputs.shape[0]

    low = jnp.concatenate([gate_weight[:, :half], up_weight[:, :half]], axis=1)
    high = jnp.concatenate([gate_weight[:, half:], up_weight[:, half:]], axis=1)
    mine, other = pick(xh, low, high)
    other = swap(other, "xh")
    first_rows, second_rows = pick(xh, mine, other)
    weights = lax.all_gather(
        jnp.concatenate([first_rows, second_rows], axis=0), "z", axis=0, tiled=True
    )

    peers = lax.axis_size(plane)
    spread = jnp.broadcast_to(inputs[None], (peers,) + inputs.shape)
    rows = lax.all_to_all(spread, plane, split_axis=0, concat_axis=0).reshape(-1, model)
    rows = jnp.concatenate([rows, swap(rows, "core")], axis=0)

    keep = keep_mask(token_key, feature_key, drop_seed)
    masked = jnp.where(keep, hidden_grad, jnp.zeros_like(hidden_grad))
    mine_grad, other_grad = pick(xh, masked[:, :half], masked[:, half:])
    other_grad = swap(other_grad, "xh")
    lower, upper = pick(xh, mine_grad, other_grad)
    kept = jnp.concatenate([lower, upper], axis=0)
    kept = kept.reshape(-1, 2, own_inputs, half)
    kept = jnp.concatenate(pick(core, kept[:, 0], kept[:, 1]), axis=0).reshape(-1, half)

    both = jnp.dot(rows, weights, preferred_element_type=f32)
    gate, up = both[:, :half], both[:, half:]
    tanh_part = jnp.tanh(gelu_coeff * (gate + 0.044715 * gate * gate * gate))
    act = 0.5 * gate * (1.0 + tanh_part)
    slope = 0.5 * (1.0 + tanh_part) + 0.5 * gate * (1.0 - tanh_part * tanh_part) * gelu_coeff * (
        1.0 + 3.0 * 0.044715 * gate * gate
    )
    dropped = kept.astype(f32) * keep_scale
    dgate = (dropped * up * slope).astype(bf16)
    dup = (dropped * act).astype(bf16)
    dboth = jnp.concatenate([dgate, dup], axis=1)

    terms = lax.dot_general(rows, dboth, (((0,), (0,)), ((), ())), preferred_element_type=f32)
    terms, dboth = lax.optimization_barrier((terms, dboth))
    terms = terms.reshape(-1, 2, own_rows, own_units)
    own_terms, partner_terms = pick(xh, terms[:, 0], terms[:, 1])
    own_sum = lax.psum_scatter(own_terms, "z", scatter_dimension=0)
    partner_sum = ring_sum(partner_terms, "z")

    partial = lax.dot_general(
        dboth, weights, (((1,), (1,)), ((), ())), preferred_element_type=f32
    )
    here = partial.shape[0] // 2
    pair = partial[:here] + swap(partial[here:], "core")
    shares = lax.all_to_all(
        pair.astype(bf16).reshape(peers, own_inputs, model), plane, split_axis=0, concat_axis=0
    )
    input_grad = jnp.sum(shares.astype(f32), axis=0).astype(bf16)

    got_sum = swap(partner_sum.astype(bf16), "xh").astype(f32)
    low_sum, high_sum = pick(xh, own_sum, got_sum)
    grad_gate = jnp.concatenate([low_sum[:, :half], high_sum[:, :half]], axis=1)
    grad_up = jnp.concatenate([low_sum[:, half:], high_sum[:, half:]], axis=1)

    gate_updated, gate_first_new, gate_second_new = adamw(
        gate_weight, gate_first, gate_second, grad_gate
    )
    up_updated, up_first_new, up_second_new = adamw(up_weight, up_first, up_second, grad_up)
    return (
        input_grad,
        gate_updated,
        up_updated,
        gate_first_new,
        gate_second_new,
        up_first_new,
        up_second_new,
    )


def solution(mesh):
    dp_size, tensor_size = mesh.devices.shape
    fine = Mesh(
        mesh.devices.reshape(dp_size // 2, 2, 2, tensor_size // 4, 2), ("z", "xh", "xl", "y", "core")
    )
    dp, tensor = ("z", "xh"), ("xl", "y", "core")
    grid = P(dp, tensor)
    every = P(dp + tensor, None)
    return jax.shard_map(
        on_device,
        mesh=fine,
        in_specs=(every, grid, P(dp), P(tensor), P()) + (grid,) * 6,
        out_specs=(every,) + (grid,) * 6,
        check_vma=False,
    )
```

```python
import functools
import math

import jax
import jax.numpy as jnp
from jax import lax
from jax.experimental import pallas as pl
from jax.experimental.pallas import tpu as pltpu
from jax.sharding import Mesh
from jax.sharding import PartitionSpec as P

drop_level = 6554
keep_scale = 65536.0 / (65536.0 - 6554.0)
gelu_coeff = math.sqrt(2.0 / math.pi)
first_fix = 1.0 - 0.9**10
second_fix = 1.0 - 0.95**10
bf16 = jnp.bfloat16
f32 = jnp.float32

plane = ("xh", "xl", "y")


def keep_mask(token_key, feature_key, drop_seed):
    mixed = (
        token_key[:, None] * -1640531535
        + feature_key[None, :] * -1028477379
        + drop_seed[0] * 668265263
    )
    mixed = mixed ^ mixed >> 15 & 131071
    mixed = mixed * -2048144789
    mixed = mixed ^ mixed >> 13 & 524287
    mixed = mixed * -1028477387
    mixed = mixed ^ mixed >> 16 & 65535
    level = mixed & 65535
    return level >= drop_level


def adamw(weight, first, second, grad):
    first_new = 0.9 * first + 0.1 * grad
    second_new = 0.95 * second + 0.05 * grad * grad
    wide = weight.astype(f32)
    step = first_new / first_fix / (jnp.sqrt(second_new / second_fix) + 1e-08) + 0.1 * wide
    return ((wide - 0.01 * step).astype(bf16), first_new, second_new)


def swap(x, axis):
    return lax.ppermute(x, axis, [(0, 1), (1, 0)])


def pick(index, first, second):
    return jnp.where(index == 0, first, second), jnp.where(index == 0, second, first)


def in_vmem(kernel, outs, name):
    def call(scalar, *arrays):
        return pl.pallas_call(
            kernel,
            out_shape=outs,
            in_specs=[pl.BlockSpec(memory_space=pltpu.SMEM)]
            + [pl.BlockSpec(memory_space=pltpu.VMEM)] * len(arrays),
            out_specs=[pl.BlockSpec(memory_space=pltpu.VMEM)] * len(outs),
            compiler_params=pltpu.CompilerParams(vmem_limit_bytes=24 * 1024 * 1024),
            name=name,
        )(scalar, *arrays)

    return call


def block_product(place_ref, step, depth, turned_ref, dboth_ref):
    size = turned_ref.shape[0] // depth
    spot = lax.rem(place_ref[0] + step % depth, depth)
    part = turned_ref[pl.ds(pl.multiple_of(spot * size, 16), size), :]
    return jnp.dot(part, dboth_ref[...], preferred_element_type=f32)


def forward_kernel(
    depth, place_ref, core_rows, other_rows, weights, kept, dboth, turned, forth, back
):
    half = kept.shape[1]
    tokens = core_rows.shape[0]
    both = []
    for j, rows in enumerate((core_rows, other_rows)):
        both.append(jnp.dot(rows[...], weights[...], preferred_element_type=f32))
        turned[:, pl.ds(j * tokens, tokens)] = rows[...].T
    for j in range(2):
        span = pl.ds(j * tokens, tokens)
        gate, up = both[j][:, :half], both[j][:, half:]
        tanh_part = jnp.tanh(gelu_coeff * (gate + 0.044715 * gate * gate * gate))
        act = 0.5 * gate * (1.0 + tanh_part)
        slope = 0.5 * (1.0 + tanh_part) + 0.5 * gate * (
            1.0 - tanh_part * tanh_part
        ) * gelu_coeff * (1.0 + 3.0 * 0.044715 * gate * gate)
        dropped = kept[span, :].astype(f32) * keep_scale
        dboth[span, :half] = (dropped * up * slope).astype(bf16)
        dboth[span, half:] = (dropped * act).astype(bf16)
    far = depth // 2
    forth[...] = block_product(place_ref, far, depth, turned, dboth).astype(bf16)
    back[...] = block_product(place_ref, far + 1, depth, turned, dboth).astype(bf16)


def hop_kernel(depth, step, place_ref, arrived, turned, dboth, total):
    term = block_product(place_ref, step, depth, turned, dboth)
    total[...] = (arrived[...].astype(f32) + term).astype(total.dtype)


def inputs_kernel(place_ref, dboth, weights, core_part, other_part):
    half = core_part.shape[0]
    over_units = (((1,), (1,)), ((), ()))
    other_part[...] = lax.dot_general(
        dboth[half:, :], weights[...], over_units, preferred_element_type=f32
    ).astype(bf16)
    core_part[...] = lax.dot_general(
        dboth[:half, :], weights[...], over_units, preferred_element_type=f32
    )


def on_device(
    inputs,
    hidden_grad,
    token_key,
    feature_key,
    drop_seed,
    gate_weight,
    up_weight,
    gate_first,
    gate_second,
    up_first,
    up_second,
):
    xh = lax.axis_index("xh")
    core = lax.axis_index("core")
    depth = lax.axis_size("z")
    own_rows, own_units = gate_weight.shape
    half = own_units // 2
    pair_rows = 2 * own_rows
    own_inputs, model = inputs.shape
    peers = lax.axis_size(plane)

    def along(x, step):
        return lax.ppermute(x, "z", [(i, (i + step) % depth) for i in range(depth)])

    def across(x, step):
        pairs = [
            (2 * i + j, 2 * ((i + step) % depth) + 1 - j) for i in range(depth) for j in range(2)
        ]
        return lax.ppermute(x, ("z", "xh"), pairs)

    low = jnp.concatenate([gate_weight[:, :half], up_weight[:, :half]], axis=1)
    high = jnp.concatenate([gate_weight[:, half:], up_weight[:, half:]], axis=1)
    mine, other = pick(xh, low, high)
    first_rows, second_rows = pick(xh, mine, swap(other, "xh"))
    weights = lax.all_gather(
        jnp.concatenate([first_rows, second_rows], axis=0), "z", axis=0, tiled=True
    )

    spread = jnp.broadcast_to(inputs[None], (peers,) + inputs.shape)
    core_rows = lax.all_to_all(spread, plane, split_axis=0, concat_axis=0).reshape(-1, model)

    keep = keep_mask(token_key, feature_key, drop_seed)
    masked = jnp.where(keep, hidden_grad, jnp.zeros_like(hidden_grad))
    mine_grad, other_grad = pick(xh, masked[:, :half], masked[:, half:])
    other_grad = swap(other_grad, "xh")
    lower, upper = pick(xh, mine_grad, other_grad)
    kept = jnp.concatenate([lower, upper], axis=0)
    kept = kept.reshape(-1, 2, own_inputs, half)
    kept = jnp.concatenate(pick(core, kept[:, 0], kept[:, 1]), axis=0).reshape(-1, half)

    core_rows, kept = lax.optimization_barrier((core_rows, kept))
    far = depth // 2
    tokens = kept.shape[0]
    place = lax.axis_index("z").reshape(1)
    block = (pair_rows, own_units)
    dboth, turned, forth, back = in_vmem(
        functools.partial(forward_kernel, depth),
        [
            jax.ShapeDtypeStruct(shape, bf16)
            for shape in ((tokens, own_units), (model, tokens), block, block)
        ],
        "forward",
    )(place, core_rows, swap(core_rows, "core"), weights, kept)

    def add_term(arrived, step, dtype=bf16):
        return in_vmem(
            functools.partial(hop_kernel, depth, step),
            [jax.ShapeDtypeStruct(block, dtype)],
            "add_term",
        )(place, arrived, turned, dboth)[0]

    core_part, other_part = in_vmem(
        inputs_kernel,
        [jax.ShapeDtypeStruct((tokens // 2, model), dtype) for dtype in (f32, bf16)],
        "inputs",
    )(place, dboth, weights)
    pair = (core_part + swap(other_part, "core").astype(f32)).astype(bf16)

    forth, back = along(forth, 1), along(back, -1)
    forth, back, pair = lax.optimization_barrier((forth, back, pair))
    shares = lax.all_to_all(
        pair.reshape(peers, own_inputs, model), plane, split_axis=0, concat_axis=0
    )
    input_grad = jnp.sum(shares.astype(f32), axis=0).astype(bf16)

    for step in range(far - 1, 1, -1):
        forth = along(add_term(forth, step), 1)
        back = along(add_term(back, 1 - step), -1)
    forth, back = add_term(forth, 1), add_term(back, 0, f32)
    own_forth, partner_forth = pick(xh, forth[:own_rows], forth[own_rows:])
    own_back, partner_back = pick(xh, back[:own_rows], back[own_rows:])
    partner_forth = across(partner_forth, 1)
    own_forth = along(own_forth, 1)
    partner_back = swap(partner_back.astype(bf16), "xh")
    input_grad, own_forth, partner_forth, partner_back = lax.optimization_barrier(
        (input_grad, own_forth, partner_forth, partner_back)
    )
    own_sum = own_forth.astype(f32) + own_back
    got_sum = partner_forth.astype(f32) + partner_back.astype(f32)

    low_sum, high_sum = pick(xh, own_sum, got_sum)
    grad_gate = jnp.concatenate([low_sum[:, :half], high_sum[:, :half]], axis=1)
    grad_up = jnp.concatenate([low_sum[:, half:], high_sum[:, half:]], axis=1)

    gate_updated, gate_first_new, gate_second_new = adamw(
        gate_weight, gate_first, gate_second, grad_gate
    )
    up_updated, up_first_new, up_second_new = adamw(up_weight, up_first, up_second, grad_up)
    return (
        input_grad,
        gate_updated,
        up_updated,
        gate_first_new,
        gate_second_new,
        up_first_new,
        up_second_new,
    )


def solution(mesh):
    dp_size, tensor_size = mesh.devices.shape
    fine = Mesh(
        mesh.devices.reshape(dp_size // 2, 2, 2, tensor_size // 4, 2), ("z", "xh", "xl", "y", "core")
    )
    dp, tensor = ("z", "xh"), ("xl", "y", "core")
    grid = P(dp, tensor)
    every = P(dp + tensor, None)
    return jax.shard_map(
        on_device,
        mesh=fine,
        in_specs=(every, grid, P(dp), P(tensor), P()) + (grid,) * 6,
        out_specs=(every,) + (grid,) * 6,
        check_vma=False,
    )
```

```python
import functools
import math

import jax
import jax.numpy as jnp
from jax import lax
from jax.experimental import pallas as pl
from jax.experimental.pallas import tpu as pltpu
from jax.sharding import Mesh
from jax.sharding import PartitionSpec as P

drop_level = 6554
keep_scale = 65536.0 / (65536.0 - 6554.0)
gelu_coeff = math.sqrt(2.0 / math.pi)
first_fix = 1.0 - 0.9**10
second_fix = 1.0 - 0.95**10
bf16 = jnp.bfloat16
f32 = jnp.float32

plane = ("xh", "xl", "y")


def keep_mask(token_key, feature_key, drop_seed):
    mixed = (
        token_key[:, None] * -1640531535
        + feature_key[None, :] * -1028477379
        + drop_seed[0] * 668265263
    )
    mixed = mixed ^ mixed >> 15 & 131071
    mixed = mixed * -2048144789
    mixed = mixed ^ mixed >> 13 & 524287
    mixed = mixed * -1028477387
    mixed = mixed ^ mixed >> 16 & 65535
    level = mixed & 65535
    return level >= drop_level


def adamw(weight, first, second, grad):
    first_new = 0.9 * first + 0.1 * grad
    second_new = 0.95 * second + 0.05 * grad * grad
    wide = weight.astype(f32)
    step = first_new / first_fix / (jnp.sqrt(second_new / second_fix) + 1e-08) + 0.1 * wide
    return ((wide - 0.01 * step).astype(bf16), first_new, second_new)


def swap(x, axis):
    return lax.ppermute(x, axis, [(0, 1), (1, 0)])


def pick(index, first, second):
    return jnp.where(index == 0, first, second), jnp.where(index == 0, second, first)


def in_vmem(kernel, outs, name):
    def call(scalar, *arrays):
        return pl.pallas_call(
            kernel,
            out_shape=outs,
            in_specs=[pl.BlockSpec(memory_space=pltpu.SMEM)]
            + [pl.BlockSpec(memory_space=pltpu.VMEM)] * len(arrays),
            out_specs=[pl.BlockSpec(memory_space=pltpu.VMEM)] * len(outs),
            compiler_params=pltpu.CompilerParams(vmem_limit_bytes=24 * 1024 * 1024),
            name=name,
        )(scalar, *arrays)

    return call


def block_product(place_ref, step, depth, turned_ref, turned_other_ref, dboth_ref):
    size = turned_ref.shape[0] // depth
    place, core = place_ref[0] >> 1, place_ref[0] & 1
    spot = lax.rem(place + (1 - 2 * core) * step + depth, depth)
    span = pl.ds(pl.multiple_of(spot * size, 16), size)
    tokens = turned_ref.shape[1]
    return jnp.dot(turned_ref[span, :], dboth_ref[:tokens, :], preferred_element_type=f32) + jnp.dot(
        turned_other_ref[span, :], dboth_ref[tokens:, :], preferred_element_type=f32
    )


def turn_kernel(place_ref, rows, turned):
    turned[...] = rows[...].T


def forward_kernel(
    depth, place_ref, turned, turned_other, weights, kept, dboth, forth, back, middle
):
    half = kept.shape[1]
    tokens = turned.shape[1]
    both = [
        lax.dot_general(
            part[...], weights[...], (((0,), (0,)), ((), ())), preferred_element_type=f32
        )
        for part in (turned, turned_other)
    ]
    for j in range(2):
        span = pl.ds(j * tokens, tokens)
        gate, up = both[j][:, :half], both[j][:, half:]
        tanh_part = jnp.tanh(gelu_coeff * (gate + 0.044715 * gate * gate * gate))
        act = 0.5 * gate * (1.0 + tanh_part)
        slope = 0.5 * (1.0 + tanh_part) + 0.5 * gate * (
            1.0 - tanh_part * tanh_part
        ) * gelu_coeff * (1.0 + 3.0 * 0.044715 * gate * gate)
        dropped = kept[span, :].astype(f32) * keep_scale
        dboth[span, :half] = (dropped * up * slope).astype(bf16)
        dboth[span, half:] = (dropped * act).astype(bf16)
    far = depth // 2
    for out, step in ((forth, far), (back, 1 - far), (middle, 0)):
        term = block_product(place_ref, step, depth, turned, turned_other, dboth)
        out[...] = term.astype(out.dtype)


def hop_kernel(depth, step, place_ref, arrived, turned, turned_other, dboth, total):
    term = block_product(place_ref, step, depth, turned, turned_other, dboth)
    total[...] = (arrived[...].astype(f32) + term).astype(total.dtype)


def inputs_kernel(place_ref, dboth, weights, core_part, other_part):
    half = core_part.shape[0]
    over_units = (((1,), (1,)), ((), ()))
    other_part[...] = lax.dot_general(
        dboth[half:, :], weights[...], over_units, preferred_element_type=f32
    ).astype(bf16)
    core_part[...] = lax.dot_general(
        dboth[:half, :], weights[...], over_units, preferred_element_type=f32
    )


def on_device(
    inputs,
    hidden_grad,
    token_key,
    feature_key,
    drop_seed,
    gate_weight,
    up_weight,
    gate_first,
    gate_second,
    up_first,
    up_second,
):
    xh = lax.axis_index("xh")
    core = lax.axis_index("core")
    depth = lax.axis_size("z")
    own_rows, own_units = gate_weight.shape
    half = own_units // 2
    pair_rows = 2 * own_rows
    own_inputs, model = inputs.shape
    peers = lax.axis_size(plane)

    def ring(x, step, turn):
        pairs = [
            ((i * 2 + j) * 2 + k, ((i + step * (1 - 2 * k)) % depth * 2 + (j ^ turn)) * 2 + k)
            for i in range(depth)
            for j in range(2)
            for k in range(2)
        ]
        return lax.ppermute(x, ("z", "xh", "core"), pairs)

    def along(x, step):
        return ring(x, step, 0)

    def across(x, step):
        return ring(x, step, 1)

    low = jnp.concatenate([gate_weight[:, :half], up_weight[:, :half]], axis=1)
    high = jnp.concatenate([gate_weight[:, half:], up_weight[:, half:]], axis=1)
    mine, other = pick(xh, low, high)
    first_rows, second_rows = pick(xh, mine, swap(other, "xh"))
    weights = lax.all_gather(
        jnp.concatenate([first_rows, second_rows], axis=0), "z", axis=0, tiled=True
    )

    spread = jnp.broadcast_to(inputs[None], (peers,) + inputs.shape)
    core_rows = lax.all_to_all(spread, plane, split_axis=0, concat_axis=0).reshape(-1, model)

    keep = keep_mask(token_key, feature_key, drop_seed)
    masked = jnp.where(keep, hidden_grad, jnp.zeros_like(hidden_grad))
    mine_grad, other_grad = pick(xh, masked[:, :half], masked[:, half:])
    other_grad = swap(other_grad, "xh")
    lower, upper = pick(xh, mine_grad, other_grad)
    kept = jnp.concatenate([lower, upper], axis=0)
    kept = kept.reshape(-1, 2, own_inputs, half)
    kept = jnp.concatenate(pick(core, kept[:, 0], kept[:, 1]), axis=0).reshape(-1, half)

    core_rows, kept = lax.optimization_barrier((core_rows, kept))
    far = depth // 2
    tokens = kept.shape[0]
    place = (2 * lax.axis_index("z") + core).reshape(1)
    block = (pair_rows, own_units)
    turn = in_vmem(turn_kernel, [jax.ShapeDtypeStruct((model, tokens // 2), bf16)], "turn")
    turned = turn(place, core_rows)[0]
    turned_other = turn(place, swap(core_rows, "core"))[0]
    dboth, forth, back, middle = in_vmem(
        functools.partial(forward_kernel, depth),
        [jax.ShapeDtypeStruct(shape, bf16) for shape in ((tokens, own_units), block, block)]
        + [jax.ShapeDtypeStruct(block, f32)],
        "forward",
    )(place, turned, turned_other, weights, kept)

    def add_term(arrived, step):
        return in_vmem(
            functools.partial(hop_kernel, depth, step),
            [jax.ShapeDtypeStruct(block, bf16)],
            "add_term",
        )(place, arrived, turned, turned_other, dboth)[0]

    core_part, other_part = in_vmem(
        inputs_kernel,
        [jax.ShapeDtypeStruct((tokens // 2, model), dtype) for dtype in (f32, bf16)],
        "inputs",
    )(place, dboth, weights)
    pair = (core_part + swap(other_part, "core").astype(f32)).astype(bf16)

    forth, back = along(forth, 1), along(back, -1)
    own_sum, partner_sum = pick(xh, middle[:own_rows], middle[own_rows:])
    got_sum = swap(partner_sum.astype(bf16), "xh")
    forth, back, pair, got_sum = lax.optimization_barrier((forth, back, pair, got_sum))
    shares = lax.all_to_all(
        pair.reshape(peers, own_inputs, model), plane, split_axis=0, concat_axis=0
    )
    input_grad = jnp.sum(shares.astype(f32), axis=0).astype(bf16)

    def last(message, step):
        own, partner = pick(xh, message[:own_rows], message[own_rows:])
        return along(own, step), across(partner, step)

    for step in range(far - 1, 1, -1):
        forth = along(add_term(forth, step), 1)
        back = add_term(back, 1 - step)
        back = along(back, -1) if step > 2 else last(back, -1)
    forth = last(add_term(forth, 1), 1)
    input_grad, *arrived = lax.optimization_barrier((input_grad, *forth, *back))
    own_forth, partner_forth, own_back, partner_back = (x.astype(f32) for x in arrived)
    own_sum = own_sum + own_forth + own_back
    got_sum = got_sum.astype(f32) + partner_forth + partner_back

    low_sum, high_sum = pick(xh, own_sum, got_sum)
    grad_gate = jnp.concatenate([low_sum[:, :half], high_sum[:, :half]], axis=1)
    grad_up = jnp.concatenate([low_sum[:, half:], high_sum[:, half:]], axis=1)

    gate_updated, gate_first_new, gate_second_new = adamw(
        gate_weight, gate_first, gate_second, grad_gate
    )
    up_updated, up_first_new, up_second_new = adamw(up_weight, up_first, up_second, grad_up)
    return (
        input_grad,
        gate_updated,
        up_updated,
        gate_first_new,
        gate_second_new,
        up_first_new,
        up_second_new,
    )


def solution(mesh):
    dp_size, tensor_size = mesh.devices.shape
    fine = Mesh(
        mesh.devices.reshape(dp_size // 2, 2, 2, tensor_size // 4, 2), ("z", "xh", "xl", "y", "core")
    )
    dp, tensor = ("z", "xh"), ("xl", "y", "core")
    grid = P(dp, tensor)
    every = P(dp + tensor, None)
    return jax.shard_map(
        on_device,
        mesh=fine,
        in_specs=(every, grid, P(dp), P(tensor), P()) + (grid,) * 6,
        out_specs=(every,) + (grid,) * 6,
        check_vma=False,
    )
```

```python
import functools
import math

import jax
import jax.numpy as jnp
from jax import lax
from jax.experimental import pallas as pl
from jax.experimental.pallas import tpu as pltpu
from jax.sharding import Mesh
from jax.sharding import PartitionSpec as P

drop_level = 6554
keep_scale = 65536.0 / (65536.0 - 6554.0)
gelu_coeff = math.sqrt(2.0 / math.pi)
first_fix = 1.0 - 0.9**10
second_fix = 1.0 - 0.95**10
bf16 = jnp.bfloat16
f32 = jnp.float32

plane = ("y", "xh", "xl")


def keep_mask(token_key, feature_key, drop_seed):
    mixed = (
        token_key[:, None] * -1640531535
        + feature_key[None, :] * -1028477379
        + drop_seed[0] * 668265263
    )
    mixed = mixed ^ mixed >> 15 & 131071
    mixed = mixed * -2048144789
    mixed = mixed ^ mixed >> 13 & 524287
    mixed = mixed * -1028477387
    mixed = mixed ^ mixed >> 16 & 65535
    level = mixed & 65535
    return level >= drop_level


def adamw(weight, first, second, grad):
    first_new = 0.9 * first + 0.1 * grad
    second_new = 0.95 * second + 0.05 * grad * grad
    wide = weight.astype(f32)
    step = first_new / first_fix / (jnp.sqrt(second_new / second_fix) + 1e-08) + 0.1 * wide
    return ((wide - 0.01 * step).astype(bf16), first_new, second_new)


def swap(x, axis):
    return lax.ppermute(x, axis, [(0, 1), (1, 0)])


def pick(index, first, second):
    return jnp.where(index == 0, first, second), jnp.where(index == 0, second, first)


def in_vmem(kernel, outs, name):
    def call(scalar, *arrays):
        return pl.pallas_call(
            kernel,
            out_shape=outs,
            in_specs=[pl.BlockSpec(memory_space=pltpu.SMEM)]
            + [pl.BlockSpec(memory_space=pltpu.VMEM)] * len(arrays),
            out_specs=[pl.BlockSpec(memory_space=pltpu.VMEM)] * len(outs),
            compiler_params=pltpu.CompilerParams(vmem_limit_bytes=24 * 1024 * 1024),
            name=name,
        )(scalar, *arrays)

    return call


def block_product(place_ref, step, depth, turned_ref, turned_other_ref, dboth_ref):
    size = turned_ref.shape[0] // depth
    place, core = place_ref[0] >> 1, place_ref[0] & 1
    spot = lax.rem(place + (1 - 2 * core) * step + depth, depth)
    span = pl.ds(pl.multiple_of(spot * size, 16), size)
    tokens = turned_ref.shape[1]
    return jnp.dot(turned_ref[span, :], dboth_ref[:tokens, :], preferred_element_type=f32) + jnp.dot(
        turned_other_ref[span, :], dboth_ref[tokens:, :], preferred_element_type=f32
    )


def turn_kernel(place_ref, rows, turned):
    turned[...] = rows[...].T


def forward_kernel(
    depth, place_ref, turned, turned_other, weights, kept, dboth, forth, back
):
    half = kept.shape[1]
    tokens = turned.shape[1]
    both = [
        lax.dot_general(
            part[...], weights[...], (((0,), (0,)), ((), ())), preferred_element_type=f32
        )
        for part in (turned, turned_other)
    ]
    for j in range(2):
        span = pl.ds(j * tokens, tokens)
        gate, up = both[j][:, :half], both[j][:, half:]
        tanh_part = jnp.tanh(gelu_coeff * (gate + 0.044715 * gate * gate * gate))
        act = 0.5 * gate * (1.0 + tanh_part)
        slope = 0.5 * (1.0 + tanh_part) + 0.5 * gate * (
            1.0 - tanh_part * tanh_part
        ) * gelu_coeff * (1.0 + 3.0 * 0.044715 * gate * gate)
        dropped = kept[span, :].astype(f32) * keep_scale
        dboth[span, :half] = (dropped * up * slope).astype(bf16)
        dboth[span, half:] = (dropped * act).astype(bf16)
    far = depth // 2
    for out, step in ((forth, far), (back, 1 - far)):
        term = block_product(place_ref, step, depth, turned, turned_other, dboth)
        out[...] = term.astype(bf16)


def middle_kernel(depth, place_ref, turned, turned_other, dboth, total):
    total[...] = block_product(place_ref, 0, depth, turned, turned_other, dboth)


def hop_kernel(depth, step, place_ref, arrived, turned, turned_other, dboth, total):
    term = block_product(place_ref, step, depth, turned, turned_other, dboth)
    total[...] = (arrived[...].astype(f32) + term).astype(total.dtype)


def inputs_kernel(place_ref, dboth, weights, core_part, other_part):
    half = core_part.shape[0]
    over_units = (((1,), (1,)), ((), ()))
    other_part[...] = lax.dot_general(
        dboth[half:, :], weights[...], over_units, preferred_element_type=f32
    ).astype(bf16)
    core_part[...] = lax.dot_general(
        dboth[:half, :], weights[...], over_units, preferred_element_type=f32
    )


def on_device(
    inputs,
    hidden_grad,
    token_key,
    feature_key,
    drop_seed,
    gate_weight,
    up_weight,
    gate_first,
    gate_second,
    up_first,
    up_second,
):
    xh = lax.axis_index("xh")
    core = lax.axis_index("core")
    depth = lax.axis_size("z")
    own_rows, own_units = gate_weight.shape
    half = own_units // 2
    pair_rows = 2 * own_rows
    own_inputs, model = inputs.shape
    peers = lax.axis_size(plane)

    def ring(x, step, turn):
        pairs = [
            ((i * 2 + j) * 2 + k, ((i + step * (1 - 2 * k)) % depth * 2 + (j ^ turn)) * 2 + k)
            for i in range(depth)
            for j in range(2)
            for k in range(2)
        ]
        return lax.ppermute(x, ("z", "xh", "core"), pairs)

    def along(x, step):
        return ring(x, step, 0)

    def across(x, step):
        return ring(x, step, 1)

    low = jnp.concatenate([gate_weight[:, :half], up_weight[:, :half]], axis=1)
    high = jnp.concatenate([gate_weight[:, half:], up_weight[:, half:]], axis=1)
    mine, other = pick(xh, low, high)
    first_rows, second_rows = pick(xh, mine, swap(other, "xh"))
    weights = lax.all_gather(
        jnp.concatenate([first_rows, second_rows], axis=0), "z", axis=0, tiled=True
    )

    spread = jnp.broadcast_to(inputs[None], (peers,) + inputs.shape)
    core_rows = lax.all_to_all(spread, plane, split_axis=0, concat_axis=0).reshape(-1, model)

    keep = keep_mask(token_key, feature_key, drop_seed)
    masked = jnp.where(keep, hidden_grad, jnp.zeros_like(hidden_grad))
    mine_grad, other_grad = pick(xh, masked[:, :half], masked[:, half:])
    other_grad = swap(other_grad, "xh")
    lower, upper = pick(xh, mine_grad, other_grad)
    across_y = lax.axis_size("y")
    kept = jnp.stack([lower, upper]).reshape(4, across_y, 2, own_inputs, half)
    kept = kept.transpose(2, 1, 0, 3, 4)
    kept = jnp.concatenate(pick(core, kept[0], kept[1]), axis=0).reshape(-1, half)

    core_rows, kept = lax.optimization_barrier((core_rows, kept))
    far = depth // 2
    tokens = kept.shape[0]
    place = (2 * lax.axis_index("z") + core).reshape(1)
    block = (pair_rows, own_units)
    turn = in_vmem(turn_kernel, [jax.ShapeDtypeStruct((model, tokens // 2), bf16)], "turn")
    turned = turn(place, core_rows)[0]
    turned_other = turn(place, swap(core_rows, "core"))[0]
    dboth, forth, back = in_vmem(
        functools.partial(forward_kernel, depth),
        [jax.ShapeDtypeStruct(shape, bf16) for shape in ((tokens, own_units), block, block)],
        "forward",
    )(place, turned, turned_other, weights, kept)

    def add_term(arrived, step):
        return in_vmem(
            functools.partial(hop_kernel, depth, step),
            [jax.ShapeDtypeStruct(block, bf16)],
            "add_term",
        )(place, arrived, turned, turned_other, dboth)[0]

    core_part, other_part = in_vmem(
        inputs_kernel,
        [jax.ShapeDtypeStruct((tokens // 2, model), dtype) for dtype in (f32, bf16)],
        "inputs",
    )(place, dboth, weights)
    pair = core_part + swap(other_part, "core").astype(f32)

    forth, back = along(forth, 1), along(back, -1)
    forth, back, pair, dboth = lax.optimization_barrier((forth, back, pair, dboth))
    columns = lax.psum_scatter(pair.reshape(across_y, -1, model), "y", scatter_dimension=0)
    middle = in_vmem(
        functools.partial(middle_kernel, depth), [jax.ShapeDtypeStruct(block, f32)], "middle"
    )(place, turned, turned_other, dboth)[0]
    own_sum, partner_sum = pick(xh, middle[:own_rows], middle[own_rows:])
    got_sum = swap(partner_sum.astype(bf16), "xh")

    def last(message, step):
        own, partner = pick(xh, message[:own_rows], message[own_rows:])
        return along(own, step), across(partner, step)

    for step in range(far - 1, 1, -1):
        forth = along(add_term(forth, step), 1)
        back = add_term(back, 1 - step)
        back = along(back, -1) if step > 2 else last(back, -1)
    forth, got_sum = lax.optimization_barrier((forth, got_sum))
    forth = last(add_term(forth, 1), 1)
    columns, *arrived = lax.optimization_barrier((columns, *forth, *back))
    shares = lax.all_to_all(
        columns.reshape(4, own_inputs, model), ("xh", "xl"), split_axis=0, concat_axis=0
    )
    input_grad = jnp.sum(shares, axis=0).astype(bf16)
    own_forth, partner_forth, own_back, partner_back = (x.astype(f32) for x in arrived)
    own_sum = own_sum + own_forth + own_back
    got_sum = got_sum.astype(f32) + partner_forth + partner_back

    low_sum, high_sum = pick(xh, own_sum, got_sum)
    grad_gate = jnp.concatenate([low_sum[:, :half], high_sum[:, :half]], axis=1)
    grad_up = jnp.concatenate([low_sum[:, half:], high_sum[:, half:]], axis=1)

    gate_updated, gate_first_new, gate_second_new = adamw(
        gate_weight, gate_first, gate_second, grad_gate
    )
    up_updated, up_first_new, up_second_new = adamw(up_weight, up_first, up_second, grad_up)
    return (
        input_grad,
        gate_updated,
        up_updated,
        gate_first_new,
        gate_second_new,
        up_first_new,
        up_second_new,
    )


def solution(mesh):
    dp_size, tensor_size = mesh.devices.shape
    fine = Mesh(
        mesh.devices.reshape(dp_size // 2, 2, 2, tensor_size // 4, 2), ("z", "xh", "xl", "y", "core")
    )
    dp, tensor = ("z", "xh"), ("xl", "y", "core")
    grid = P(dp, tensor)
    every = P(dp + tensor, None)
    return jax.shard_map(
        on_device,
        mesh=fine,
        in_specs=(every, grid, P(dp), P(tensor), P()) + (grid,) * 6,
        out_specs=(every,) + (grid,) * 6,
        check_vma=False,
    )
```

```python
import functools
import math

import jax
import jax.numpy as jnp
from jax import lax
from jax.experimental import pallas as pl
from jax.experimental.pallas import tpu as pltpu
from jax.sharding import Mesh
from jax.sharding import PartitionSpec as P

drop_level = 6554
keep_scale = 65536.0 / (65536.0 - 6554.0)
gelu_coeff = math.sqrt(2.0 / math.pi)
first_fix = 1.0 - 0.9**10
second_fix = 1.0 - 0.95**10
bf16 = jnp.bfloat16
f32 = jnp.float32

plane = ("y", "xh", "xl")


def keep_mask(token_key, feature_key, drop_seed):
    mixed = (
        token_key[:, None] * -1640531535
        + feature_key[None, :] * -1028477379
        + drop_seed[0] * 668265263
    )
    mixed = mixed ^ mixed >> 15 & 131071
    mixed = mixed * -2048144789
    mixed = mixed ^ mixed >> 13 & 524287
    mixed = mixed * -1028477387
    mixed = mixed ^ mixed >> 16 & 65535
    level = mixed & 65535
    return level >= drop_level


def adamw(weight, first, second, grad):
    first_new = 0.9 * first + 0.1 * grad
    second_new = 0.95 * second + 0.05 * grad * grad
    wide = weight.astype(f32)
    step = first_new / first_fix / (jnp.sqrt(second_new / second_fix) + 1e-08) + 0.1 * wide
    return ((wide - 0.01 * step).astype(bf16), first_new, second_new)


def swap(x, axis):
    return lax.ppermute(x, axis, [(0, 1), (1, 0)])


def pick(index, first, second):
    return jnp.where(index == 0, first, second), jnp.where(index == 0, second, first)


def in_vmem(kernel, outs, name, scratch=()):
    def call(scalar, *arrays):
        return pl.pallas_call(
            kernel,
            out_shape=outs,
            in_specs=[pl.BlockSpec(memory_space=pltpu.SMEM)]
            + [pl.BlockSpec(memory_space=pltpu.VMEM)] * len(arrays),
            out_specs=[pl.BlockSpec(memory_space=pltpu.VMEM)] * len(outs),
            scratch_shapes=scratch,
            compiler_params=pltpu.CompilerParams(vmem_limit_bytes=24 * 1024 * 1024),
            name=name,
        )(scalar, *arrays)

    return call


def block_product(place_ref, step, depth, turned_ref, turned_other_ref, dboth_ref):
    size = turned_ref.shape[0] // depth
    place, core = place_ref[0] >> 2, place_ref[0] >> 1 & 1
    spot = lax.rem(place + (1 - 2 * core) * step + depth, depth)
    span = pl.ds(pl.multiple_of(spot * size, 16), size)
    tokens = turned_ref.shape[1]
    return jnp.dot(turned_ref[span, :], dboth_ref[:tokens, :], preferred_element_type=f32) + jnp.dot(
        turned_other_ref[span, :], dboth_ref[tokens:, :], preferred_element_type=f32
    )


def turn_kernel(place_ref, rows, turned):
    turned[...] = rows[...].T


def forward_kernel(
    depth, place_ref, turned, turned_other, weights, kept, dboth, forth, back
):
    half = kept.shape[1]
    tokens = turned.shape[1]
    both = [
        lax.dot_general(
            part[...], weights[...], (((0,), (0,)), ((), ())), preferred_element_type=f32
        )
        for part in (turned, turned_other)
    ]
    for j in range(2):
        span = pl.ds(j * tokens, tokens)
        gate, up = both[j][:, :half], both[j][:, half:]
        tanh_part = jnp.tanh(gelu_coeff * (gate + 0.044715 * gate * gate * gate))
        act = 0.5 * gate * (1.0 + tanh_part)
        slope = 0.5 * (1.0 + tanh_part) + 0.5 * gate * (
            1.0 - tanh_part * tanh_part
        ) * gelu_coeff * (1.0 + 3.0 * 0.044715 * gate * gate)
        dropped = kept[span, :].astype(f32) * keep_scale
        dboth[span, :half] = (dropped * up * slope).astype(bf16)
        dboth[span, half:] = (dropped * act).astype(bf16)
    far = depth // 2
    for out, step in ((forth, far), (back, 1 - far)):
        term = block_product(place_ref, step, depth, turned, turned_other, dboth)
        out[...] = term.astype(bf16)


def halves_of(place_ref, rows):
    xh = place_ref[0] & 1
    return pl.ds(pl.multiple_of(xh * rows, 16), rows), pl.ds(
        pl.multiple_of((1 - xh) * rows, 16), rows
    )


def hop_kernel(depth, step, place_ref, arrived, turned, turned_other, dboth, total):
    term = block_product(place_ref, step, depth, turned, turned_other, dboth)
    total[...] = (arrived[...].astype(f32) + term).astype(total.dtype)


def hop_with_own_kernel(
    depth, step, place_ref, arrived, turned, turned_other, dboth, total, own_sum, scratch
):
    size, rows = arrived.shape[0], own_sum.shape[0]
    term = block_product(place_ref, step, depth, turned, turned_other, dboth)
    total[:size, :] = (arrived[...].astype(f32) + term).astype(bf16)
    scratch[...] = block_product(place_ref, 0, depth, turned, turned_other, dboth)
    own, partner = halves_of(place_ref, rows)
    own_sum[...] = scratch[own, :]
    total[size:, :] = scratch[partner, :].astype(bf16)


def last_hop_kernel(
    depth, step, place_ref, arrived, turned, turned_other, dboth, *refs
):
    *extra, own_out, partner_out, scratch = refs
    size, rows = scratch.shape[0], own_out.shape[0]
    term = block_product(place_ref, step, depth, turned, turned_other, dboth)
    scratch[...] = arrived[:size, :].astype(f32) + term
    own, partner = halves_of(place_ref, rows)
    own_out[...] = scratch[own, :].astype(bf16)
    total = scratch[partner, :]
    for ref in extra:
        total = total + ref[size:, :].astype(f32)
    partner_out[...] = total.astype(bf16)


def inputs_kernel(half, place_ref, dboth, weights, out):
    tokens = out.shape[0]
    out[...] = lax.dot_general(
        dboth[half * tokens : (half + 1) * tokens, :],
        weights[...],
        (((1,), (1,)), ((), ())),
        preferred_element_type=f32,
    ).astype(out.dtype)


def on_device(
    inputs,
    hidden_grad,
    token_key,
    feature_key,
    drop_seed,
    gate_weight,
    up_weight,
    gate_first,
    gate_second,
    up_first,
    up_second,
):
    xh = lax.axis_index("xh")
    core = lax.axis_index("core")
    depth = lax.axis_size("z")
    own_rows, own_units = gate_weight.shape
    half = own_units // 2
    pair_rows = 2 * own_rows
    own_inputs, model = inputs.shape
    peers = lax.axis_size(plane)

    def ring(x, step, turn):
        pairs = [
            ((i * 2 + j) * 2 + k, ((i + step * (1 - 2 * k)) % depth * 2 + (j ^ turn)) * 2 + k)
            for i in range(depth)
            for j in range(2)
            for k in range(2)
        ]
        return lax.ppermute(x, ("z", "xh", "core"), pairs)

    def along(x, step):
        return ring(x, step, 0)

    def across(x, step):
        return ring(x, step, 1)

    low = jnp.concatenate([gate_weight[:, :half], up_weight[:, :half]], axis=1)
    high = jnp.concatenate([gate_weight[:, half:], up_weight[:, half:]], axis=1)
    mine, other = pick(xh, low, high)
    first_rows, second_rows = pick(xh, mine, swap(other, "xh"))
    weights = lax.all_gather(
        jnp.concatenate([first_rows, second_rows], axis=0), "z", axis=0, tiled=True
    )

    spread = jnp.broadcast_to(inputs[None], (peers,) + inputs.shape)
    core_rows = lax.all_to_all(spread, plane, split_axis=0, concat_axis=0).reshape(-1, model)

    keep = keep_mask(token_key, feature_key, drop_seed)
    masked = jnp.where(keep, hidden_grad, jnp.zeros_like(hidden_grad))
    mine_grad, other_grad = pick(xh, masked[:, :half], masked[:, half:])
    other_grad = swap(other_grad, "xh")
    lower, upper = pick(xh, mine_grad, other_grad)
    across_y = lax.axis_size("y")
    kept = jnp.stack([lower, upper]).reshape(4, across_y, 2, own_inputs, half)
    kept = kept.transpose(2, 1, 0, 3, 4)
    kept = jnp.concatenate(pick(core, kept[0], kept[1]), axis=0).reshape(-1, half)

    core_rows, kept = lax.optimization_barrier((core_rows, kept))
    far = depth // 2
    tokens = kept.shape[0]
    place = (4 * lax.axis_index("z") + 2 * core + xh).reshape(1)
    block = (pair_rows, own_units)
    turn = in_vmem(turn_kernel, [jax.ShapeDtypeStruct((model, tokens // 2), bf16)], "turn")
    turned = turn(place, core_rows)[0]
    turned_other = turn(place, swap(core_rows, "core"))[0]
    dboth, forth, back = in_vmem(
        functools.partial(forward_kernel, depth),
        [jax.ShapeDtypeStruct(shape, bf16) for shape in ((tokens, own_units), block, block)],
        "forward",
    )(place, turned, turned_other, weights, kept)

    rows_block, wide = (own_rows, own_units), pltpu.VMEM(block, f32)

    def hop(kernel, step, outs, scratch, arrived, *extra):
        return in_vmem(
            functools.partial(kernel, depth, step),
            [jax.ShapeDtypeStruct(shape, dtype) for shape, dtype in outs],
            "hop",
            scratch,
        )(place, arrived, turned, turned_other, dboth, *extra)

    def add_term(arrived, step):
        return hop(hop_kernel, step, [(block, bf16)], (), arrived)[0]

    def last(arrived, step, way, *extra):
        outs = [(rows_block, bf16)] * 2
        own, partner = hop(last_hop_kernel, step, outs, [wide], arrived, *extra)
        return along(own, way), across(partner, way)

    def back_product(part, dtype):
        return in_vmem(
            functools.partial(inputs_kernel, part),
            [jax.ShapeDtypeStruct((tokens // 2, model), dtype)],
            "inputs",
        )(place, dboth, weights)[0]

    other_part = swap(back_product(1, bf16), "core")
    pair = back_product(0, f32) + other_part.astype(f32)

    forth, back = along(forth, 1), along(back, -1)
    forth, back, dboth = lax.optimization_barrier((forth, back, dboth))
    columns = lax.psum_scatter(pair.reshape(across_y, -1, model), "y", scatter_dimension=0)
    forth = along(add_term(forth, far - 1), 1)
    message = (pair_rows + own_rows, own_units)
    back, own_sum = hop(
        hop_with_own_kernel, 2 - far, [(message, bf16), (rows_block, f32)], [wide], back
    )
    back = along(back, -1)
    returned = back
    for step in range(far - 2, 1, -1):
        forth = along(add_term(forth, step), 1)
        back = last(back, 1 - step, -1) if step == 2 else along(add_term(back, 1 - step), -1)
    forth = last(forth, 1, 1, returned)
    columns, *back = lax.optimization_barrier((columns, *back))
    shares = lax.all_to_all(
        columns.reshape(4, own_inputs, model), ("xh", "xl"), split_axis=0, concat_axis=0
    )
    input_grad = jnp.sum(shares, axis=0).astype(bf16)
    own_forth, partner_forth, own_back, partner_back = (x.astype(f32) for x in (*forth, *back))
    own_sum = own_sum + own_forth + own_back
    got_sum = partner_forth + partner_back

    low_sum, high_sum = pick(xh, own_sum, got_sum)
    grad_gate = jnp.concatenate([low_sum[:, :half], high_sum[:, :half]], axis=1)
    grad_up = jnp.concatenate([low_sum[:, half:], high_sum[:, half:]], axis=1)

    gate_updated, gate_first_new, gate_second_new = adamw(
        gate_weight, gate_first, gate_second, grad_gate
    )
    up_updated, up_first_new, up_second_new = adamw(up_weight, up_first, up_second, grad_up)
    return (
        input_grad,
        gate_updated,
        up_updated,
        gate_first_new,
        gate_second_new,
        up_first_new,
        up_second_new,
    )


def solution(mesh):
    dp_size, tensor_size = mesh.devices.shape
    fine = Mesh(
        mesh.devices.reshape(dp_size // 2, 2, 2, tensor_size // 4, 2), ("z", "xh", "xl", "y", "core")
    )
    dp, tensor = ("z", "xh"), ("xl", "y", "core")
    grid = P(dp, tensor)
    every = P(dp + tensor, None)
    return jax.shard_map(
        on_device,
        mesh=fine,
        in_specs=(every, grid, P(dp), P(tensor), P()) + (grid,) * 6,
        out_specs=(every,) + (grid,) * 6,
        check_vma=False,
    )
```

```python
import functools
import math

import jax
import jax.numpy as jnp
from jax import lax
from jax.experimental import pallas as pl
from jax.experimental.pallas import tpu as pltpu
from jax.sharding import Mesh
from jax.sharding import PartitionSpec as P

drop_level = 6554
keep_scale = 65536.0 / (65536.0 - 6554.0)
gelu_coeff = math.sqrt(2.0 / math.pi)
first_fix = 1.0 - 0.9**10
second_fix = 1.0 - 0.95**10
bf16 = jnp.bfloat16
f32 = jnp.float32

plane = ("y", "xh", "xl")


def keep_mask(token_key, feature_key, drop_seed):
    mixed = (
        token_key[:, None] * -1640531535
        + feature_key[None, :] * -1028477379
        + drop_seed[0] * 668265263
    )
    mixed = mixed ^ mixed >> 15 & 131071
    mixed = mixed * -2048144789
    mixed = mixed ^ mixed >> 13 & 524287
    mixed = mixed * -1028477387
    mixed = mixed ^ mixed >> 16 & 65535
    level = mixed & 65535
    return level >= drop_level


def adamw(weight, first, second, grad):
    first_new = 0.9 * first + 0.1 * grad
    second_new = 0.95 * second + 0.05 * grad * grad
    wide = weight.astype(f32)
    step = first_new / first_fix / (jnp.sqrt(second_new / second_fix) + 1e-08) + 0.1 * wide
    return ((wide - 0.01 * step).astype(bf16), first_new, second_new)


def swap(x, axis):
    return lax.ppermute(x, axis, [(0, 1), (1, 0)])


def pick(index, first, second):
    return jnp.where(index == 0, first, second), jnp.where(index == 0, second, first)


def in_vmem(kernel, outs, name, scratch=()):
    def call(scalar, *arrays):
        return pl.pallas_call(
            kernel,
            out_shape=outs,
            in_specs=[pl.BlockSpec(memory_space=pltpu.SMEM)]
            + [pl.BlockSpec(memory_space=pltpu.VMEM)] * len(arrays),
            out_specs=[pl.BlockSpec(memory_space=pltpu.VMEM)] * len(outs),
            scratch_shapes=scratch,
            compiler_params=pltpu.CompilerParams(vmem_limit_bytes=24 * 1024 * 1024),
            name=name,
        )(scalar, *arrays)

    return call


def block_product(place_ref, step, depth, turned_ref, turned_other_ref, dboth_ref):
    size = turned_ref.shape[0] // depth
    place, core = place_ref[0] >> 2, place_ref[0] >> 1 & 1
    spot = lax.rem(place + (1 - 2 * core) * step + depth, depth)
    span = pl.ds(pl.multiple_of(spot * size, 16), size)
    tokens = turned_ref.shape[1]
    return jnp.dot(turned_ref[span, :], dboth_ref[:tokens, :], preferred_element_type=f32) + jnp.dot(
        turned_other_ref[span, :], dboth_ref[tokens:, :], preferred_element_type=f32
    )


def turn_kernel(place_ref, rows, turned):
    turned[...] = rows[...].T


def forward_kernel(place_ref, turned, turned_other, weights, kept, dboth):
    half = kept.shape[1]
    tokens = turned.shape[1]
    both = [
        lax.dot_general(
            part[...], weights[...], (((0,), (0,)), ((), ())), preferred_element_type=f32
        )
        for part in (turned, turned_other)
    ]
    for j in range(2):
        span = pl.ds(j * tokens, tokens)
        gate, up = both[j][:, :half], both[j][:, half:]
        tanh_part = jnp.tanh(gelu_coeff * (gate + 0.044715 * gate * gate * gate))
        act = 0.5 * gate * (1.0 + tanh_part)
        slope = 0.5 * (1.0 + tanh_part) + 0.5 * gate * (
            1.0 - tanh_part * tanh_part
        ) * gelu_coeff * (1.0 + 3.0 * 0.044715 * gate * gate)
        dropped = kept[span, :].astype(f32) * keep_scale
        dboth[span, :half] = (dropped * up * slope).astype(bf16)
        dboth[span, half:] = (dropped * act).astype(bf16)


def begin_kernel(depth, place_ref, turned, turned_other, dboth, forth, back):
    far = depth // 2
    for out, step in ((forth, far), (back, 1 - far)):
        out[...] = block_product(place_ref, step, depth, turned, turned_other, dboth).astype(bf16)


def halves_of(place_ref, rows):
    xh = place_ref[0] & 1
    return pl.ds(pl.multiple_of(xh * rows, 16), rows), pl.ds(
        pl.multiple_of((1 - xh) * rows, 16), rows
    )


def hop_kernel(depth, step, place_ref, arrived, turned, turned_other, dboth, total):
    term = block_product(place_ref, step, depth, turned, turned_other, dboth)
    total[...] = (arrived[...].astype(f32) + term).astype(total.dtype)


def hop_with_own_kernel(
    depth, step, place_ref, arrived, turned, turned_other, dboth, total, own_sum, scratch
):
    size, rows = arrived.shape[0], own_sum.shape[0]
    term = block_product(place_ref, step, depth, turned, turned_other, dboth)
    total[:size, :] = (arrived[...].astype(f32) + term).astype(bf16)
    scratch[...] = block_product(place_ref, 0, depth, turned, turned_other, dboth)
    own, partner = halves_of(place_ref, rows)
    own_sum[...] = scratch[own, :]
    total[size:, :] = scratch[partner, :].astype(bf16)


def last_hop_kernel(
    depth, step, place_ref, arrived, turned, turned_other, dboth, *refs
):
    *extra, own_out, partner_out, scratch = refs
    size, rows = scratch.shape[0], own_out.shape[0]
    term = block_product(place_ref, step, depth, turned, turned_other, dboth)
    scratch[...] = arrived[:size, :].astype(f32) + term
    own, partner = halves_of(place_ref, rows)
    own_out[...] = scratch[own, :].astype(bf16)
    total = scratch[partner, :]
    for ref in extra:
        total = total + ref[size:, :].astype(f32)
    partner_out[...] = total.astype(bf16)


def inputs_kernel(half, place_ref, dboth, weights, out):
    tokens = out.shape[0]
    out[...] = lax.dot_general(
        dboth[half * tokens : (half + 1) * tokens, :],
        weights[...],
        (((1,), (1,)), ((), ())),
        preferred_element_type=f32,
    ).astype(out.dtype)


def on_device(
    inputs,
    hidden_grad,
    token_key,
    feature_key,
    drop_seed,
    gate_weight,
    up_weight,
    gate_first,
    gate_second,
    up_first,
    up_second,
):
    xh = lax.axis_index("xh")
    core = lax.axis_index("core")
    depth = lax.axis_size("z")
    own_rows, own_units = gate_weight.shape
    half = own_units // 2
    pair_rows = 2 * own_rows
    own_inputs, model = inputs.shape
    peers = lax.axis_size(plane)

    def ring(x, step, turn):
        pairs = [
            ((i * 2 + j) * 2 + k, ((i + step * (1 - 2 * k)) % depth * 2 + (j ^ turn)) * 2 + k)
            for i in range(depth)
            for j in range(2)
            for k in range(2)
        ]
        return lax.ppermute(x, ("z", "xh", "core"), pairs)

    def along(x, step):
        return ring(x, step, 0)

    def across(x, step):
        return ring(x, step, 1)

    low = jnp.concatenate([gate_weight[:, :half], up_weight[:, :half]], axis=1)
    high = jnp.concatenate([gate_weight[:, half:], up_weight[:, half:]], axis=1)
    mine, other = pick(xh, low, high)
    first_rows, second_rows = pick(xh, mine, swap(other, "xh"))
    weights = lax.all_gather(
        jnp.concatenate([first_rows, second_rows], axis=0), "z", axis=0, tiled=True
    )

    spread = jnp.broadcast_to(inputs[None], (peers,) + inputs.shape)
    core_rows = lax.all_to_all(spread, plane, split_axis=0, concat_axis=0).reshape(-1, model)

    keep = keep_mask(token_key, feature_key, drop_seed)
    masked = jnp.where(keep, hidden_grad, jnp.zeros_like(hidden_grad))
    mine_grad, other_grad = pick(xh, masked[:, :half], masked[:, half:])
    other_grad = swap(other_grad, "xh")
    lower, upper = pick(xh, mine_grad, other_grad)
    across_y = lax.axis_size("y")
    kept = jnp.stack([lower, upper]).reshape(4, across_y, 2, own_inputs, half)
    kept = kept.transpose(2, 1, 0, 3, 4)
    kept = jnp.concatenate(pick(core, kept[0], kept[1]), axis=0).reshape(-1, half)

    core_rows, kept = lax.optimization_barrier((core_rows, kept))
    far = depth // 2
    tokens = kept.shape[0]
    place = (4 * lax.axis_index("z") + 2 * core + xh).reshape(1)
    block = (pair_rows, own_units)
    turn = in_vmem(turn_kernel, [jax.ShapeDtypeStruct((model, tokens // 2), bf16)], "turn")
    turned = turn(place, core_rows)[0]
    turned_other = turn(place, swap(core_rows, "core"))[0]
    dboth = in_vmem(
        forward_kernel, [jax.ShapeDtypeStruct((tokens, own_units), bf16)], "forward"
    )(place, turned, turned_other, weights, kept)[0]
    forth, back = in_vmem(
        functools.partial(begin_kernel, depth), [jax.ShapeDtypeStruct(block, bf16)] * 2, "begin"
    )(place, turned, turned_other, dboth)

    rows_block, wide = (own_rows, own_units), pltpu.VMEM(block, f32)

    def hop(kernel, step, outs, scratch, arrived, *extra):
        return in_vmem(
            functools.partial(kernel, depth, step),
            [jax.ShapeDtypeStruct(shape, dtype) for shape, dtype in outs],
            "hop",
            scratch,
        )(place, arrived, turned, turned_other, dboth, *extra)

    def add_term(arrived, step):
        return hop(hop_kernel, step, [(block, bf16)], (), arrived)[0]

    def last(arrived, step, way, *extra):
        outs = [(rows_block, bf16)] * 2
        own, partner = hop(last_hop_kernel, step, outs, [wide], arrived, *extra)
        return along(own, way), across(partner, way)

    def back_product(part, dtype):
        return in_vmem(
            functools.partial(inputs_kernel, part),
            [jax.ShapeDtypeStruct((tokens // 2, model), dtype)],
            "inputs",
        )(place, dboth, weights)[0]

    other_part = swap(back_product(1, bf16), "core")
    pair = back_product(0, f32) + other_part.astype(f32)

    forth, back = along(forth, 1), along(back, -1)
    columns = lax.psum_scatter(pair.reshape(across_y, -1, model), "y", scatter_dimension=0)
    forth = along(add_term(forth, far - 1), 1)
    message = (pair_rows + own_rows, own_units)
    back, own_sum = hop(
        hop_with_own_kernel, 2 - far, [(message, bf16), (rows_block, f32)], [wide], back
    )
    back = along(back, -1)
    returned = back
    for step in range(far - 2, 1, -1):
        forth = along(add_term(forth, step), 1)
        back = last(back, 1 - step, -1) if step == 2 else along(add_term(back, 1 - step), -1)
    forth = last(forth, 1, 1, returned)
    columns, *back = lax.optimization_barrier((columns, *back))
    shares = lax.all_to_all(
        columns.reshape(4, own_inputs, model), ("xh", "xl"), split_axis=0, concat_axis=0
    )
    input_grad = jnp.sum(shares, axis=0).astype(bf16)
    own_forth, partner_forth, own_back, partner_back = (x.astype(f32) for x in (*forth, *back))
    own_sum = own_sum + own_forth + own_back
    got_sum = partner_forth + partner_back

    low_sum, high_sum = pick(xh, own_sum, got_sum)
    grad_gate = jnp.concatenate([low_sum[:, :half], high_sum[:, :half]], axis=1)
    grad_up = jnp.concatenate([low_sum[:, half:], high_sum[:, half:]], axis=1)

    gate_updated, gate_first_new, gate_second_new = adamw(
        gate_weight, gate_first, gate_second, grad_gate
    )
    up_updated, up_first_new, up_second_new = adamw(up_weight, up_first, up_second, grad_up)
    return (
        input_grad,
        gate_updated,
        up_updated,
        gate_first_new,
        gate_second_new,
        up_first_new,
        up_second_new,
    )


def solution(mesh):
    dp_size, tensor_size = mesh.devices.shape
    fine = Mesh(
        mesh.devices.reshape(dp_size // 2, 2, 2, tensor_size // 4, 2), ("z", "xh", "xl", "y", "core")
    )
    dp, tensor = ("z", "xh"), ("xl", "y", "core")
    grid = P(dp, tensor)
    every = P(dp + tensor, None)
    return jax.shard_map(
        on_device,
        mesh=fine,
        in_specs=(every, grid, P(dp), P(tensor), P()) + (grid,) * 6,
        out_specs=(every,) + (grid,) * 6,
        check_vma=False,
    )
```
